32 devices in a mesh: section: 4 (over y, x), shard: 2 (over core), tensor: 4 (over z).
Axes of the slice: x: 2, y: 2, z: 4, core: 2. Of those that a mesh axis runs over, the one named last changes fastest.
Arguments:
- grad_terms: float32 [4, 2, 5120, 1280], P('section', 'shard', 'tensor'), may hold values from -5 to 5
- weights: bfloat16 [4, 4, 1280, 1280], P('section', 'tensor', 'shard'), may hold values from -4 to 4
- basis: float32 [4, 1280, 256], P('section'), may hold values from -5 to 5
- first_moment: float32 [4, 4, 1280, 256], P('section', 'tensor', 'shard'), may hold values from -4 to 4
- second_moment: float32 [4, 4, 1280, 256], P('section', 'tensor', 'shard'), may hold values from 0.1 to 2
Outputs:
- new_weights: bfloat16 [4, 4, 1280, 1280], P('section', 'tensor', 'shard')
- new_first: float32 [4, 4, 1280, 256], P('section', 'tensor', 'shard')
- new_second: float32 [4, 4, 1280, 256], P('section', 'tensor', 'shard')
- new_basis: float32 [4, 1280, 256], P('section')
The draws below stay inside these ranges and needn't reach their ends.
All inputs are finite; a program needn't handle non-finite values.
Results may differ from the reference program's by a relative error of at most 0.001.
Values sent between devices are 32-bit elements; how exact they have to be, the bound alone decides.
A program may use at most 64 MiB of HBM per device.

```python
import math
import jax
import jax.numpy as jnp
from jax import lax

D = 1280
FF = 5120
R = 256
NS_STEPS = 5
LAYERS = 4
N_SHARD = 2
N_TENSOR = 4


def strengthened(entries, own_key, source, target, shards_of, factor):
    def block_of(axis_at):
        return (jnp.arange(entries.shape[axis_at]) // (entries.shape[axis_at] // shards_of)).reshape((-1,) + (1,) * (entries.ndim - 1 - axis_at))

    near = jax.random.permutation(own_key, shards_of)[block_of(target)]
    second = (block_of(target) + shards_of // 2) % shards_of
    return jnp.where((block_of(source) == near) | (block_of(source) == second), factor * entries, entries)


def block_levels(stream_key, shape, shards, low, high):
    gain, own = 1.0, jax.random.fold_in(stream_key, 6)
    for position, blocks in shards:
        draws = jnp.exp(jax.random.uniform(jax.random.fold_in(own, position), (blocks,), jnp.float32, low / len(shards), high / len(shards)))
        gain = gain * jnp.repeat(draws, shape[position] // blocks).reshape([-1 if axis == position else 1 for axis in range(len(shape))])
    return gain


def gaussian(stream_key, extent, scale, most, cuts=(), dtype=jnp.bfloat16):
    entries = scale * jax.random.normal(stream_key, extent, jnp.float32)
    if cuts:
        entries = entries * block_levels(stream_key, extent, cuts, -0.22, 0.18)
    return jnp.clip(entries, -most, most).astype(dtype)


def bell_draw_with(key, extent, spread, reach, shards, heavy, dtype=jnp.bfloat16):
    drawn = spread * jax.random.normal(key, extent, jnp.float32)
    if shards:
        drawn = drawn * block_levels(key, extent, shards, -0.22, 0.18)
    return jnp.clip(strengthened(drawn, jax.random.fold_in(key, 3), *heavy), -reach, reach).astype(dtype)


def setup_inputs(seed: int = 0) -> dict:
    keys = jax.random.split(jax.random.key(seed), 6)
    return {
        "grad_terms": bell_draw_with(keys[0], (LAYERS, N_SHARD, FF, D), 0.25, 5.0, ((0, 4), (1, 2), (2, 4)), (1, 2, 2, 2.0), jnp.float32),
        "weights": gaussian(keys[1], (LAYERS, N_TENSOR, FF // N_TENSOR, D), 1.0, 4.0, ((0, 4), (1, 4), (2, 2))),
        "basis": gaussian(keys[2], (LAYERS, D, R), 1.0, 5.0, ((0, 4),), jnp.float32),
        "first_moment": gaussian(keys[3], (LAYERS, N_TENSOR, FF // N_TENSOR, R), 0.5, 4.0, ((0, 4), (1, 4), (2, 2)), jnp.float32),
        "second_moment": jnp.clip(jnp.exp(math.log(2.0) - 2.9957323 * jax.random.uniform(keys[4], (LAYERS, N_TENSOR, FF // N_TENSOR, R), jnp.float32) ** block_levels(keys[4], (LAYERS, N_TENSOR, FF // N_TENSOR, R), ((0, 4), (1, 4), (2, 2)), -0.2, 0.2)), 0.1, 2.0),
    }


def matmul(left, right):
    return jnp.dot(left, right, precision=lax.Precision.HIGHEST, preferred_element_type=jnp.float32)

def inner_rows(left, right):
    return lax.dot_general(left, right, (((0,), (0,)), ((), ())), precision=lax.Precision.HIGHEST, preferred_element_type=jnp.float32)

def local_gram(iterate):
    return inner_rows(iterate, iterate)

def newton_steps(power):
    gram_now = local_gram(power)
    scaling = lax.rsqrt(jnp.trace(gram_now) + 1e-06)
    iterate = power * scaling
    gram_now = gram_now * (scaling * scaling)
    for sweep in range(NS_STEPS):
        iterate = 1.5 * iterate - 0.5 * matmul(iterate, gram_now)
        if sweep + 1 < NS_STEPS:
            gram_now = local_gram(iterate)
    return iterate

def reference(grad_terms, weights, basis, first_moment, second_moment):
    root_width = math.sqrt(D)
    weight_list, first_list, second_list, basis_list = ([], [], [], [])
    for layer in range(LAYERS):
        gradient = lax.optimization_barrier(jnp.sum(grad_terms[layer], axis=0))
        basis_now = basis[layer]
        low_rank = matmul(gradient, basis_now) / root_width
        moment_one = 0.9 * first_moment[layer].reshape(FF, R) + 0.1 * low_rank
        moment_two = 0.95 * second_moment[layer].reshape(FF, R) + 0.05 * low_rank * low_rank
        direction = moment_one / (jnp.sqrt(moment_two) + 1e-08)
        update = lax.dot_general(direction, basis_now, (((1,), (1,)), ((), ())), precision=lax.Precision.HIGHEST, preferred_element_type=jnp.float32)
        stepped = weights[layer].reshape(FF, D).astype(jnp.float32) - 0.5 * update / root_width
        normed = stepped * lax.rsqrt(lax.optimization_barrier(jnp.mean(stepped * stepped, axis=1, keepdims=True)) + 1e-06)
        power = inner_rows(gradient, low_rank)
        iterate = newton_steps(power)
        weight_list.append(normed.astype(jnp.bfloat16).reshape(N_TENSOR, FF // N_TENSOR, D))
        first_list.append(moment_one.reshape(N_TENSOR, FF // N_TENSOR, R))
        second_list.append(moment_two.reshape(N_TENSOR, FF // N_TENSOR, R))
        basis_list.append(iterate * root_width)
    return (jnp.stack(weight_list), jnp.stack(first_list), jnp.stack(second_list), jnp.stack(basis_list))
```

```python
import functools
import math

import jax
import jax.numpy as jnp
from jax import lax
from jax.experimental import pallas as pl
from jax.experimental.pallas import tpu as pltpu
from jax.sharding import PartitionSpec as P

NS_STEPS = 5
MESH = pl.DeviceIdType.MESH
F32 = jnp.float32
BF16 = jnp.bfloat16
NN = ((1,), (0,))
NT = ((1,), (1,))
TILE = 256
SUBS = 2
SKEW = 2
VMEM_LIMIT = 56 * 1024 * 1024


def split(value):
    high = value.astype(BF16)
    return high, (value - high.astype(F32)).astype(BF16)


def dot3(left, right, dims):
    def one(a, b):
        return lax.dot_general(a, b, (dims, ((), ())), preferred_element_type=F32)

    return one(left[0], right[0]) + (one(left[0], right[1]) + one(left[1], right[0]))


def reduce_kernel(
    n_tensor,
    grad_hbm,
    basis_hbm,
    weight_hbm,
    first_hbm,
    second_hbm,
    weight_out,
    first_out,
    second_out,
    power_out,
    gram_out,
    grad,
    grad_high,
    grad_low,
    basis,
    basis_high,
    basis_low,
    low_mine,
    low_other,
    low_full,
    turned_high,
    turned_low,
    weight,
    first,
    second,
    part,
    part_other,
    own,
    pre_in,
    suf_in,
    pre_out,
    suf_out,
    total,
    in_sem,
    grad_sem,
    low_send,
    low_recv,
    part_send,
    part_recv,
    pre_send,
    pre_recv,
    suf_send,
    suf_recv,
    tot_send,
    tot_recv,
    out_sem,
):
    rows, width = grad.shape
    rank = basis.shape[1]
    half_rows = weight.shape[0]
    half_rank = rank // 2
    sub_rank = half_rank // SUBS
    row_tiles, col_tiles = rows // TILE, width // TILE
    pieces = col_tiles * SUBS
    root_width = math.sqrt(width)
    core = lax.axis_index("shard")
    other = 1 - core
    here = lax.axis_index("tensor")
    has_left, has_right = here > 0, here < n_tensor - 1

    def grad_copy(i):
        at = pl.ds(pl.multiple_of(i * TILE, TILE), TILE)
        return pltpu.make_async_copy(grad_hbm.at[at], grad.at[at], grad_sem.at[i])

    basis_copy = pltpu.make_async_copy(basis_hbm, basis, in_sem.at[0])
    basis_copy.start()
    for i in range(row_tiles):
        grad_copy(i).start()
    state_copies = [
        pltpu.make_async_copy(first_hbm, first, in_sem.at[1]),
        pltpu.make_async_copy(second_hbm, second, in_sem.at[2]),
        pltpu.make_async_copy(weight_hbm, weight, in_sem.at[3]),
    ]
    for copy in state_copies:
        copy.start()

    barrier = pltpu.get_barrier_semaphore()
    pl.semaphore_signal(barrier, inc=1, device_id={"shard": other}, device_id_type=MESH)

    @pl.when(has_left)
    def _():
        pl.semaphore_signal(barrier, inc=1, device_id={"tensor": here - 1}, device_id_type=MESH)

    @pl.when(has_right)
    def _():
        pl.semaphore_signal(barrier, inc=1, device_id={"tensor": here + 1}, device_id_type=MESH)

    basis_copy.wait()
    high, low = split(basis[...])
    basis_high[...] = high
    basis_low[...] = low

    pl.semaphore_wait(barrier, 1 + has_left.astype(jnp.int32) + has_right.astype(jnp.int32))

    def low_copy(i):
        at = pl.ds(pl.multiple_of(i * TILE, TILE), TILE)
        return pltpu.make_async_remote_copy(
            src_ref=low_mine.at[at],
            dst_ref=low_other.at[at],
            send_sem=low_send.at[i],
            recv_sem=low_recv.at[i],
            device_id={"shard": other},
            device_id_type=MESH,
        )

    def project(i, _):
        at = pl.ds(pl.multiple_of(i * TILE, TILE), TILE)
        grad_copy(i).wait()
        pair = split(grad[at, :])
        grad_high[at, :] = pair[0]
        grad_low[at, :] = pair[1]
        low_mine[at, :] = dot3(pair, (basis_high[...], basis_low[...]), NN)
        low_copy(i).start()
        return 0

    lax.fori_loop(0, row_tiles, project, 0)

    def join(i, _):
        at = pl.ds(pl.multiple_of(i * TILE, TILE), TILE)
        low_copy(i).wait_recv()
        block = (low_mine[at, :] + low_other[at, :]) * (1.0 / root_width)
        low_full[at, :] = block
        pair = split(block.T)
        turned_high[:, at] = pair[0]
        turned_low[:, at] = pair[1]
        return 0

    lax.fori_loop(0, row_tiles, join, 0)

    def part_copy(d):
        return pltpu.make_async_remote_copy(
            src_ref=part.at[d, pl.ds(pl.multiple_of(other * half_rank, half_rank), half_rank)],
            dst_ref=part_other.at[d],
            send_sem=part_send.at[d],
            recv_sem=part_recv.at[d],
            device_id={"shard": other},
            device_id_type=MESH,
        )

    def line_copy(source, target, k, send, recv, device):
        return pltpu.make_async_remote_copy(
            src_ref=source.at[k],
            dst_ref=target.at[k],
            send_sem=send.at[k],
            recv_sem=recv.at[k],
            device_id={"tensor": device},
            device_id_type=MESH,
        )

    def pre_copy(source, k):
        return line_copy(source, pre_in, k, pre_send, pre_recv, here + 1)

    def suf_copy(source, k):
        return line_copy(source, suf_in, k, suf_send, suf_recv, here - 1)

    def settle(d):
        part_copy(d).wait_recv()
        for s in range(SUBS):
            k = d * SUBS + s
            mine = pl.ds(pl.multiple_of(core * half_rank + s * sub_rank, sub_rank), sub_rank)
            own[k] = part[d, mine, :] + part_other[d, s * sub_rank : (s + 1) * sub_rank, :]

            @pl.when(jnp.logical_not(has_left))
            def _():
                pre_copy(own, k).start()

            @pl.when(jnp.logical_not(has_right))
            def _():
                suf_copy(own, k).start()

    def power_tile(d, _):
        at = pl.ds(pl.multiple_of(d * TILE, TILE), TILE)
        part[d] = dot3(
            (turned_high[...], turned_low[...]), (grad_high[:, at], grad_low[:, at]), NN
        )
        part_copy(d).start()

        @pl.when(d >= 1)
        def _():
            settle(d - 1)

        return 0

    lax.fori_loop(0, col_tiles, power_tile, 0)
    settle(col_tiles - 1)
    for copy in state_copies:
        copy.wait()

    def forward_pre(k):
        @pl.when(has_left)
        def _():
            pre_copy(pre_out, k).wait_recv()

            @pl.when(has_right)
            def _():
                pre_out[k] = pre_in[k] + own[k]
                pre_copy(pre_out, k).start()

    def forward_suf(k):
        @pl.when(has_right)
        def _():
            suf_copy(suf_out, k).wait_recv()

            @pl.when(has_left)
            def _():
                suf_out[k] = suf_in[k] + own[k]
                suf_copy(suf_out, k).start()

    def total_copy(k):
        d, s = k // SUBS, k % SUBS
        at = pl.ds(pl.multiple_of(core * half_rank + s * sub_rank, sub_rank), sub_rank)
        return pltpu.make_async_remote_copy(
            src_ref=total.at[d, at],
            dst_ref=total.at[d, at],
            send_sem=tot_send.at[k],
            recv_sem=tot_recv.at[k],
            device_id={"shard": other},
            device_id_type=MESH,
        )

    def finish(k):
        d, s = k // SUBS, k % SUBS
        at = pl.ds(pl.multiple_of(core * half_rank + s * sub_rank, sub_rank), sub_rank)

        @pl.when(jnp.logical_not(has_left))
        def _():
            total[d, at, :] = own[k] + suf_in[k]

        @pl.when(jnp.logical_not(has_right))
        def _():
            total[d, at, :] = own[k] + pre_in[k]

        @pl.when(jnp.logical_and(has_left, has_right))
        def _():
            total[d, at, :] = own[k] + (pre_in[k] + suf_in[k])

        total_copy(k).start()

    step_rows = half_rows // col_tiles

    def state_copy_out(source, target, j, which):
        at = pl.ds(pl.multiple_of(j * step_rows, 16), step_rows)
        return pltpu.make_async_copy(source.at[at], target.at[at], out_sem.at[which, j])

    def out_copies(j):
        return [
            state_copy_out(weight, weight_out, j, 0),
            state_copy_out(first, first_out, j, 1),
            state_copy_out(second, second_out, j, 2),
        ]

    def update_rows(j):
        at = pl.ds(pl.multiple_of(j * step_rows, 16), step_rows)
        low_rank = low_full[pl.ds(pl.multiple_of(core * half_rows + j * step_rows, 16), step_rows), :]
        moment_one = 0.9 * first[at, :] + 0.1 * low_rank
        moment_two = 0.95 * second[at, :] + 0.05 * low_rank * low_rank
        first[at, :] = moment_one
        second[at, :] = moment_two
        direction = moment_one / (jnp.sqrt(moment_two) + 1e-08)
        update = dot3(split(direction), (basis_high[...], basis_low[...]), NT)
        stepped = weight[at, :].astype(F32) - (0.5 / root_width) * update
        mean = jnp.mean(stepped * stepped, axis=1, keepdims=True)
        weight[at, :] = (stepped * lax.rsqrt(mean + 1e-06)).astype(BF16)
        for copy in out_copies(j):
            copy.start()

    gram_out[...] = jnp.zeros_like(gram_out)

    def gram_tile(d):
        for s in range(SUBS):
            total_copy(d * SUBS + s).wait_recv()
        block = total[d]
        pair = split(block)
        gram_out[...] += dot3(pair, pair, NT)
        power_out[pl.ds(pl.multiple_of(d * TILE, TILE), TILE), :] = block.T

    left_side = 2 * here < n_tensor

    def line_step(step, _):
        @pl.when(step < pieces)
        def _():
            @pl.when(left_side)
            def _():
                forward_pre(step)

            @pl.when(jnp.logical_not(left_side))
            def _():
                forward_suf(step)

        @pl.when(step >= SKEW)
        def _():
            k = step - SKEW

            @pl.when(left_side)
            def _():
                forward_suf(k)

            @pl.when(jnp.logical_not(left_side))
            def _():
                forward_pre(k)

            finish(k)

            @pl.when(jnp.logical_and(k % SUBS == SUBS - 1, k >= 2 * SUBS - 1))
            def _():
                gram_tile(k // SUBS - 1)

        @pl.when(jnp.logical_and(step % SUBS == 0, step < pieces))
        def _():
            update_rows(step // SUBS)

        return 0

    lax.fori_loop(0, pieces + SKEW, line_step, 0)
    gram_tile(col_tiles - 1)

    def drain(d, _):
        low_copy(d).wait_send()
        part_copy(d).wait_send()
        for copy in out_copies(d):
            copy.wait()
        for s in range(SUBS):
            k = d * SUBS + s
            total_copy(k).wait_send()

            @pl.when(has_right)
            def _():
                pre_copy(pre_out, k).wait_send()

            @pl.when(has_left)
            def _():
                suf_copy(suf_out, k).wait_send()

        return 0

    lax.fori_loop(0, col_tiles, drain, 0)


def newton_scale(gram, dot):
    size = gram.shape[0]
    rows = lax.broadcasted_iota(jnp.int32, (size, size), 0)
    columns = lax.broadcasted_iota(jnp.int32, (size, size), 1)
    eye = jnp.where(rows == columns, 1.0, 0.0).astype(F32)
    scaling = lax.rsqrt(jnp.sum(gram * eye) + 1e-06)
    now = gram * (scaling * scaling)
    product = None
    for sweep in range(NS_STEPS):
        factor = 1.5 * eye - 0.5 * now
        if sweep + 1 < NS_STEPS:
            now = dot(dot(now, factor), factor)
        product = factor if product is None else dot(product, factor)
    return product, scaling


def finish_kernel(
    power_ref, gram_ref, weight_in, first_in, second_in,
    weight_out, first_out, second_out, basis_out, sem,
):
    copies = [
        pltpu.make_async_copy(weight_in, weight_out, sem.at[0]),
        pltpu.make_async_copy(first_in, first_out, sem.at[1]),
        pltpu.make_async_copy(second_in, second_out, sem.at[2]),
    ]
    for copy in copies:
        copy.start()
    product, scaling = newton_scale(
        gram_ref[...], lambda a, b: dot3(split(a), split(b), NN)
    )
    product = split(product * (scaling * math.sqrt(power_ref.shape[0])))
    for d in range(power_ref.shape[0] // TILE):
        at = pl.ds(d * TILE, TILE)
        basis_out[at, :] = dot3(split(power_ref[at, :]), product, NN)
    for copy in copies:
        copy.wait()


def fused_device(n_tensor, grad_terms, weights, basis, first_moment, second_moment):
    rows, width = grad_terms.shape[2:]
    rank = basis.shape[2]
    half_rows = rows // 2
    tiles = width // TILE
    row_tiles = rows // TILE
    pieces = tiles * SUBS
    piece = (pieces, rank // 2 // SUBS, TILE)
    hbm = pl.BlockSpec(memory_space=pl.ANY)
    vmem = pl.BlockSpec(memory_space=pltpu.VMEM)
    dma = pltpu.SemaphoreType.DMA
    state = [
        jax.ShapeDtypeStruct((half_rows, width), BF16),
        jax.ShapeDtypeStruct((half_rows, rank), F32),
        jax.ShapeDtypeStruct((half_rows, rank), F32),
    ]
    new_weights, new_first, new_second, power, gram = pl.pallas_call(
        functools.partial(reduce_kernel, n_tensor),
        out_shape=state
        + [
            jax.ShapeDtypeStruct((width, rank), F32),
            jax.ShapeDtypeStruct((rank, rank), F32),
        ],
        in_specs=[hbm] * 5,
        out_specs=[hbm, hbm, hbm, vmem, vmem],
        scratch_shapes=[
            pltpu.VMEM((rows, width), F32),
            pltpu.VMEM((rows, width), BF16),
            pltpu.VMEM((rows, width), BF16),
            pltpu.VMEM((width, rank), F32),
            pltpu.VMEM((width, rank), BF16),
            pltpu.VMEM((width, rank), BF16),
            pltpu.VMEM((rows, rank), F32),
            pltpu.VMEM((rows, rank), F32),
            pltpu.VMEM((rows, rank), F32),
            pltpu.VMEM((rank, rows), BF16),
            pltpu.VMEM((rank, rows), BF16),
            pltpu.VMEM((half_rows, width), BF16),
            pltpu.VMEM((half_rows, rank), F32),
            pltpu.VMEM((half_rows, rank), F32),
            pltpu.VMEM((tiles, rank, TILE), F32),
            pltpu.VMEM((tiles, rank // 2, TILE), F32),
            pltpu.VMEM(piece, F32),
            pltpu.VMEM(piece, F32),
            pltpu.VMEM(piece, F32),
            pltpu.VMEM(piece, F32),
            pltpu.VMEM(piece, F32),
            pltpu.VMEM((tiles, rank, TILE), F32),
            dma((4,)),
            dma((row_tiles,)),
            dma((row_tiles,)),
            dma((row_tiles,)),
            dma((tiles,)),
            dma((tiles,)),
            dma((pieces,)),
            dma((pieces,)),
            dma((pieces,)),
            dma((pieces,)),
            dma((pieces,)),
            dma((pieces,)),
            dma((3, tiles)),
        ],
        compiler_params=pltpu.CompilerParams(
            collective_id=0, has_side_effects=True, vmem_limit_bytes=VMEM_LIMIT
        ),
        name="reduce",
    )(grad_terms[0, 0], basis[0], weights[0, 0], first_moment[0, 0], second_moment[0, 0])
    new_weights, new_first, new_second, new_basis = pl.pallas_call(
        finish_kernel,
        out_shape=state + [jax.ShapeDtypeStruct((width, rank), F32)],
        in_specs=[vmem, vmem, hbm, hbm, hbm],
        out_specs=[hbm, hbm, hbm, vmem],
        scratch_shapes=[dma((3,))],
        compiler_params=pltpu.CompilerParams(vmem_limit_bytes=VMEM_LIMIT),
        name="finish",
    )(power, gram, new_weights, new_first, new_second)
    return (
        new_weights[None, None],
        new_first[None, None],
        new_second[None, None],
        new_basis[None],
    )


def dot_high(left, right, dims=NN):
    return lax.dot_general(
        left, right, (dims, ((), ())), precision=lax.Precision.HIGH, preferred_element_type=F32
    )


def plain_device(grad_terms, weights, basis, first_moment, second_moment):
    basis_now = basis[0]
    root_width = math.sqrt(basis_now.shape[0])
    grad_rows = lax.psum_scatter(grad_terms[0, 0], "shard", scatter_dimension=0, tiled=True)
    low_rank = dot_high(grad_rows, basis_now) / root_width
    power_part = dot_high(grad_rows, low_rank, ((0,), (0,)))
    power = lax.psum(power_part, ("shard", "tensor"))
    moment_one = 0.9 * first_moment[0, 0] + 0.1 * low_rank
    moment_two = 0.95 * second_moment[0, 0] + 0.05 * low_rank * low_rank
    direction = moment_one / (jnp.sqrt(moment_two) + 1e-08)
    update = dot_high(direction, basis_now, NT)
    stepped = weights[0, 0].astype(F32) - 0.5 * update / root_width
    normed = stepped * lax.rsqrt(jnp.mean(stepped * stepped, axis=1, keepdims=True) + 1e-06)
    product, scaling = newton_scale(dot_high(power, power, ((0,), (0,))), dot_high)
    new_basis = dot_high(power, product) * (scaling * root_width)
    return (
        normed.astype(BF16)[None, None],
        moment_one[None, None],
        moment_two[None, None],
        new_basis[None],
    )


def solution(mesh):
    n_shard, n_tensor = mesh.shape["shard"], mesh.shape["tensor"]

    def per_device(grad_terms, weights, basis, first_moment, second_moment):
        args = (grad_terms, weights, basis, first_moment, second_moment)
        if n_shard == 2 and n_tensor > 1:
            return fused_device(n_tensor, *args)
        return plain_device(*args)

    return jax.shard_map(
        per_device,
        mesh=mesh,
        in_specs=(
            P("section", "shard", "tensor", None),
            P("section", "tensor", "shard", None),
            P("section", None, None),
            P("section", "tensor", "shard", None),
            P("section", "tensor", "shard", None),
        ),
        out_specs=(
            P("section", "tensor", "shard", None),
            P("section", "tensor", "shard", None),
            P("section", "tensor", "shard", None),
            P("section", None, None),
        ),
        check_vma=False,
    )
```

```python
import functools
import math

import jax
import jax.numpy as jnp
from jax import lax
from jax.experimental import pallas as pl
from jax.experimental.pallas import tpu as pltpu
from jax.sharding import PartitionSpec as P

NS_STEPS = 5
MESH = pl.DeviceIdType.MESH
F32 = jnp.float32
BF16 = jnp.bfloat16
NN = ((1,), (0,))
NT = ((1,), (1,))
TILE = 256
SUBS = 2
SKEW = 3
VMEM_LIMIT = 56 * 1024 * 1024


def split(value):
    high = value.astype(BF16)
    return high, (value - high.astype(F32)).astype(BF16)


def dot3(left, right, dims):
    def one(a, b):
        return lax.dot_general(a, b, (dims, ((), ())), preferred_element_type=F32)

    return one(left[0], right[0]) + (one(left[0], right[1]) + one(left[1], right[0]))


def reduce_kernel(
    n_tensor,
    grad_hbm,
    basis_hbm,
    weight_hbm,
    first_hbm,
    second_hbm,
    weight_out,
    first_out,
    second_out,
    power_out,
    gram_out,
    grad,
    grad_high,
    grad_low,
    basis,
    basis_high,
    basis_low,
    low_mine,
    low_other,
    low_full,
    turned_high,
    turned_low,
    weight,
    first,
    second,
    part,
    part_other,
    own,
    pre_in,
    suf_in,
    pre_out,
    suf_out,
    total,
    in_sem,
    grad_sem,
    low_send,
    low_recv,
    part_send,
    part_recv,
    pre_send,
    pre_recv,
    suf_send,
    suf_recv,
    tot_send,
    tot_recv,
    out_sem,
):
    rows, width = grad.shape
    rank = basis.shape[1]
    half_rows = weight.shape[0]
    half_rank = rank // 2
    sub_rank = half_rank // SUBS
    row_tiles, col_tiles = rows // TILE, width // TILE
    pieces = col_tiles * SUBS
    root_width = math.sqrt(width)
    core = lax.axis_index("shard")
    other = 1 - core
    here = lax.axis_index("tensor")
    has_left, has_right = here > 0, here < n_tensor - 1

    def grad_copy(i):
        at = pl.ds(pl.multiple_of(i * TILE, TILE), TILE)
        return pltpu.make_async_copy(grad_hbm.at[at], grad.at[at], grad_sem.at[i])

    basis_copy = pltpu.make_async_copy(basis_hbm, basis, in_sem.at[0])
    basis_copy.start()
    for i in range(row_tiles):
        grad_copy(i).start()
    state_copies = [
        pltpu.make_async_copy(first_hbm, first, in_sem.at[1]),
        pltpu.make_async_copy(second_hbm, second, in_sem.at[2]),
        pltpu.make_async_copy(weight_hbm, weight, in_sem.at[3]),
    ]
    for copy in state_copies:
        copy.start()

    barrier = pltpu.get_barrier_semaphore()
    pl.semaphore_signal(barrier, inc=1, device_id={"shard": other}, device_id_type=MESH)

    @pl.when(has_left)
    def _():
        pl.semaphore_signal(barrier, inc=1, device_id={"tensor": here - 1}, device_id_type=MESH)

    @pl.when(has_right)
    def _():
        pl.semaphore_signal(barrier, inc=1, device_id={"tensor": here + 1}, device_id_type=MESH)

    basis_copy.wait()
    high, low = split(basis[...])
    basis_high[...] = high
    basis_low[...] = low

    pl.semaphore_wait(barrier, 1 + has_left.astype(jnp.int32) + has_right.astype(jnp.int32))

    def low_copy(i):
        at = pl.ds(pl.multiple_of(i * TILE, TILE), TILE)
        return pltpu.make_async_remote_copy(
            src_ref=low_mine.at[at],
            dst_ref=low_other.at[at],
            send_sem=low_send.at[i],
            recv_sem=low_recv.at[i],
            device_id={"shard": other},
            device_id_type=MESH,
        )

    def project(i, _):
        at = pl.ds(pl.multiple_of(i * TILE, TILE), TILE)
        grad_copy(i).wait()
        pair = split(grad[at, :])
        grad_high[at, :] = pair[0]
        grad_low[at, :] = pair[1]
        low_mine[at, :] = dot3(pair, (basis_high[...], basis_low[...]), NN)
        low_copy(i).start()
        return 0

    lax.fori_loop(0, row_tiles, project, 0)

    def join(i, _):
        at = pl.ds(pl.multiple_of(i * TILE, TILE), TILE)
        low_copy(i).wait_recv()
        block = (low_mine[at, :] + low_other[at, :]) * (1.0 / root_width)
        low_full[at, :] = block
        pair = split(block.T)
        turned_high[:, at] = pair[0]
        turned_low[:, at] = pair[1]
        return 0

    lax.fori_loop(0, row_tiles, join, 0)

    def part_copy(d):
        return pltpu.make_async_remote_copy(
            src_ref=part.at[d, pl.ds(pl.multiple_of(other * half_rank, half_rank), half_rank)],
            dst_ref=part_other.at[d],
            send_sem=part_send.at[d],
            recv_sem=part_recv.at[d],
            device_id={"shard": other},
            device_id_type=MESH,
        )

    def line_copy(source, target, k, send, recv, device):
        return pltpu.make_async_remote_copy(
            src_ref=source.at[k],
            dst_ref=target.at[k],
            send_sem=send.at[k],
            recv_sem=recv.at[k],
            device_id={"tensor": device},
            device_id_type=MESH,
        )

    def pre_copy(source, k):
        return line_copy(source, pre_in, k, pre_send, pre_recv, here + 1)

    def suf_copy(source, k):
        return line_copy(source, suf_in, k, suf_send, suf_recv, here - 1)

    def settle(d):
        part_copy(d).wait_recv()
        for s in range(SUBS):
            k = d * SUBS + s
            mine = pl.ds(pl.multiple_of(core * half_rank + s * sub_rank, sub_rank), sub_rank)
            own[k] = part[d, mine, :] + part_other[d, s * sub_rank : (s + 1) * sub_rank, :]

            @pl.when(jnp.logical_not(has_left))
            def _():
                pre_copy(own, k).start()

            @pl.when(jnp.logical_not(has_right))
            def _():
                suf_copy(own, k).start()

    def power_tile(d, _):
        at = pl.ds(pl.multiple_of(d * TILE, TILE), TILE)
        part[d] = dot3(
            (turned_high[...], turned_low[...]), (grad_high[:, at], grad_low[:, at]), NN
        )
        part_copy(d).start()

        @pl.when(d >= 1)
        def _():
            settle(d - 1)

        return 0

    lax.fori_loop(0, col_tiles, power_tile, 0)
    settle(col_tiles - 1)
    for copy in state_copies:
        copy.wait()

    def forward_pre(k):
        @pl.when(has_left)
        def _():
            pre_copy(pre_out, k).wait_recv()

            @pl.when(has_right)
            def _():
                pre_out[k] = pre_in[k] + own[k]
                pre_copy(pre_out, k).start()

    def forward_suf(k):
        @pl.when(has_right)
        def _():
            suf_copy(suf_out, k).wait_recv()

            @pl.when(has_left)
            def _():
                suf_out[k] = suf_in[k] + own[k]
                suf_copy(suf_out, k).start()

    def total_copy(k):
        d, s = k // SUBS, k % SUBS
        at = pl.ds(pl.multiple_of(core * half_rank + s * sub_rank, sub_rank), sub_rank)
        return pltpu.make_async_remote_copy(
            src_ref=total.at[d, at],
            dst_ref=total.at[d, at],
            send_sem=tot_send.at[k],
            recv_sem=tot_recv.at[k],
            device_id={"shard": other},
            device_id_type=MESH,
        )

    def finish(k):
        d, s = k // SUBS, k % SUBS
        at = pl.ds(pl.multiple_of(core * half_rank + s * sub_rank, sub_rank), sub_rank)

        @pl.when(jnp.logical_not(has_left))
        def _():
            total[d, at, :] = own[k] + suf_in[k]

        @pl.when(jnp.logical_not(has_right))
        def _():
            total[d, at, :] = own[k] + pre_in[k]

        @pl.when(jnp.logical_and(has_left, has_right))
        def _():
            total[d, at, :] = own[k] + (pre_in[k] + suf_in[k])

        total_copy(k).start()

    step_rows = half_rows // col_tiles

    def state_copy_out(source, target, j, which):
        at = pl.ds(pl.multiple_of(j * step_rows, 16), step_rows)
        return pltpu.make_async_copy(source.at[at], target.at[at], out_sem.at[which, j])

    def out_copies(j):
        return [
            state_copy_out(weight, weight_out, j, 0),
            state_copy_out(first, first_out, j, 1),
            state_copy_out(second, second_out, j, 2),
        ]

    def update_rows(j):
        at = pl.ds(pl.multiple_of(j * step_rows, 16), step_rows)
        low_rank = low_full[pl.ds(pl.multiple_of(core * half_rows + j * step_rows, 16), step_rows), :]
        moment_one = 0.9 * first[at, :] + 0.1 * low_rank
        moment_two = 0.95 * second[at, :] + 0.05 * low_rank * low_rank
        first[at, :] = moment_one
        second[at, :] = moment_two
        direction = moment_one / (jnp.sqrt(moment_two) + 1e-08)
        update = dot3(split(direction), (basis_high[...], basis_low[...]), NT)
        stepped = weight[at, :].astype(F32) - (0.5 / root_width) * update
        mean = jnp.mean(stepped * stepped, axis=1, keepdims=True)
        weight[at, :] = (stepped * lax.rsqrt(mean + 1e-06)).astype(BF16)
        for copy in out_copies(j):
            copy.start()

    gram_out[...] = jnp.zeros_like(gram_out)

    def gram_tile(d):
        for s in range(SUBS):
            total_copy(d * SUBS + s).wait_recv()
        block = total[d]
        pair = split(block)
        gram_out[...] += dot3(pair, pair, NT)
        power_out[pl.ds(pl.multiple_of(d * TILE, TILE), TILE), :] = block.T

    left_side = 2 * here < n_tensor

    def line_step(step, _):
        @pl.when(step < pieces)
        def _():
            @pl.when(left_side)
            def _():
                forward_pre(step)

            @pl.when(jnp.logical_not(left_side))
            def _():
                forward_suf(step)

        @pl.when(step >= SKEW)
        def _():
            k = step - SKEW

            @pl.when(left_side)
            def _():
                forward_suf(k)

            @pl.when(jnp.logical_not(left_side))
            def _():
                forward_pre(k)

            finish(k)

            @pl.when(jnp.logical_and(k % SUBS == SUBS - 1, k >= 2 * SUBS - 1))
            def _():
                gram_tile(k // SUBS - 1)

        @pl.when(jnp.logical_and(step % SUBS == 0, step < pieces))
        def _():
            update_rows(step // SUBS)

        return 0

    lax.fori_loop(0, pieces + SKEW, line_step, 0)
    gram_tile(col_tiles - 1)

    def drain(d, _):
        low_copy(d).wait_send()
        part_copy(d).wait_send()
        for copy in out_copies(d):
            copy.wait()
        for s in range(SUBS):
            k = d * SUBS + s
            total_copy(k).wait_send()

            @pl.when(has_right)
            def _():
                pre_copy(pre_out, k).wait_send()

            @pl.when(has_left)
            def _():
                suf_copy(suf_out, k).wait_send()

        return 0

    lax.fori_loop(0, col_tiles, drain, 0)


def newton_scale(gram, dot, between=None):
    size = gram.shape[0]
    rows = lax.broadcasted_iota(jnp.int32, (size, size), 0)
    columns = lax.broadcasted_iota(jnp.int32, (size, size), 1)
    eye = jnp.where(rows == columns, 1.0, 0.0).astype(F32)
    scaling = lax.rsqrt(jnp.sum(gram * eye) + 1e-06)
    now = gram * (scaling * scaling)
    product = None
    for sweep in range(NS_STEPS):
        factor = 1.5 * eye - 0.5 * now
        if sweep == 2 and between is not None:
            between()
        if sweep + 1 < NS_STEPS:
            now = dot(dot(now, factor), factor)
        product = factor if product is None else dot(product, factor)
    return product, scaling


def finish_kernel(
    power_ref, gram_ref, weight_in, first_in, second_in,
    weight_out, first_out, second_out, basis_out, weight, first, second, in_sem, out_sem,
):
    held = ((weight_in, weight, weight_out), (first_in, first, first_out), (second_in, second, second_out))
    loads = [pltpu.make_async_copy(a, b, in_sem.at[i]) for i, (a, b, _) in enumerate(held)]
    stores = [pltpu.make_async_copy(b, c, out_sem.at[i]) for i, (_, b, c) in enumerate(held)]
    for copy in loads:
        copy.start()

    def pass_on():
        for load, store in zip(loads, stores):
            load.wait()
            store.start()

    product, scaling = newton_scale(
        gram_ref[...], lambda a, b: dot3(split(a), split(b), NN), pass_on
    )
    product = split(product * (scaling * math.sqrt(power_ref.shape[0])))
    for d in range(power_ref.shape[0] // TILE):
        at = pl.ds(d * TILE, TILE)
        basis_out[at, :] = dot3(split(power_ref[at, :]), product, NN)
    for copy in stores:
        copy.wait()


def fused_device(n_tensor, grad_terms, weights, basis, first_moment, second_moment):
    rows, width = grad_terms.shape[2:]
    rank = basis.shape[2]
    half_rows = rows // 2
    tiles = width // TILE
    row_tiles = rows // TILE
    pieces = tiles * SUBS
    piece = (pieces, rank // 2 // SUBS, TILE)
    hbm = pl.BlockSpec(memory_space=pl.ANY)
    vmem = pl.BlockSpec(memory_space=pltpu.VMEM)
    dma = pltpu.SemaphoreType.DMA
    state = [
        jax.ShapeDtypeStruct((half_rows, width), BF16),
        jax.ShapeDtypeStruct((half_rows, rank), F32),
        jax.ShapeDtypeStruct((half_rows, rank), F32),
    ]
    new_weights, new_first, new_second, power, gram = pl.pallas_call(
        functools.partial(reduce_kernel, n_tensor),
        out_shape=state
        + [
            jax.ShapeDtypeStruct((width, rank), F32),
            jax.ShapeDtypeStruct((rank, rank), F32),
        ],
        in_specs=[hbm] * 5,
        out_specs=[hbm, hbm, hbm, vmem, vmem],
        scratch_shapes=[
            pltpu.VMEM((rows, width), F32),
            pltpu.VMEM((rows, width), BF16),
            pltpu.VMEM((rows, width), BF16),
            pltpu.VMEM((width, rank), F32),
            pltpu.VMEM((width, rank), BF16),
            pltpu.VMEM((width, rank), BF16),
            pltpu.VMEM((rows, rank), F32),
            pltpu.VMEM((rows, rank), F32),
            pltpu.VMEM((rows, rank), F32),
            pltpu.VMEM((rank, rows), BF16),
            pltpu.VMEM((rank, rows), BF16),
            pltpu.VMEM((half_rows, width), BF16),
            pltpu.VMEM((half_rows, rank), F32),
            pltpu.VMEM((half_rows, rank), F32),
            pltpu.VMEM((tiles, rank, TILE), F32),
            pltpu.VMEM((tiles, rank // 2, TILE), F32),
            pltpu.VMEM(piece, F32),
            pltpu.VMEM(piece, F32),
            pltpu.VMEM(piece, F32),
            pltpu.VMEM(piece, F32),
            pltpu.VMEM(piece, F32),
            pltpu.VMEM((tiles, rank, TILE), F32),
            dma((4,)),
            dma((row_tiles,)),
            dma((row_tiles,)),
            dma((row_tiles,)),
            dma((tiles,)),
            dma((tiles,)),
            dma((pieces,)),
            dma((pieces,)),
            dma((pieces,)),
            dma((pieces,)),
            dma((pieces,)),
            dma((pieces,)),
            dma((3, tiles)),
        ],
        compiler_params=pltpu.CompilerParams(
            collective_id=0, has_side_effects=True, vmem_limit_bytes=VMEM_LIMIT
        ),
        name="reduce",
    )(grad_terms[0, 0], basis[0], weights[0, 0], first_moment[0, 0], second_moment[0, 0])
    new_weights, new_first, new_second, new_basis = pl.pallas_call(
        finish_kernel,
        out_shape=state + [jax.ShapeDtypeStruct((width, rank), F32)],
        in_specs=[vmem, vmem, hbm, hbm, hbm],
        out_specs=[hbm, hbm, hbm, vmem],
        scratch_shapes=[
            pltpu.VMEM((half_rows, width), BF16),
            pltpu.VMEM((half_rows, rank), F32),
            pltpu.VMEM((half_rows, rank), F32),
            dma((3,)),
            dma((3,)),
        ],
        compiler_params=pltpu.CompilerParams(vmem_limit_bytes=VMEM_LIMIT),
        name="finish",
    )(power, gram, new_weights, new_first, new_second)
    return (
        new_weights[None, None],
        new_first[None, None],
        new_second[None, None],
        new_basis[None],
    )


def dot_high(left, right, dims=NN):
    return lax.dot_general(
        left, right, (dims, ((), ())), precision=lax.Precision.HIGH, preferred_element_type=F32
    )


def plain_device(grad_terms, weights, basis, first_moment, second_moment):
    basis_now = basis[0]
    root_width = math.sqrt(basis_now.shape[0])
    grad_rows = lax.psum_scatter(grad_terms[0, 0], "shard", scatter_dimension=0, tiled=True)
    low_rank = dot_high(grad_rows, basis_now) / root_width
    power_part = dot_high(grad_rows, low_rank, ((0,), (0,)))
    power = lax.psum(power_part, ("shard", "tensor"))
    moment_one = 0.9 * first_moment[0, 0] + 0.1 * low_rank
    moment_two = 0.95 * second_moment[0, 0] + 0.05 * low_rank * low_rank
    direction = moment_one / (jnp.sqrt(moment_two) + 1e-08)
    update = dot_high(direction, basis_now, NT)
    stepped = weights[0, 0].astype(F32) - 0.5 * update / root_width
    normed = stepped * lax.rsqrt(jnp.mean(stepped * stepped, axis=1, keepdims=True) + 1e-06)
    product, scaling = newton_scale(dot_high(power, power, ((0,), (0,))), dot_high)
    new_basis = dot_high(power, product) * (scaling * root_width)
    return (
        normed.astype(BF16)[None, None],
        moment_one[None, None],
        moment_two[None, None],
        new_basis[None],
    )


def solution(mesh):
    n_shard, n_tensor = mesh.shape["shard"], mesh.shape["tensor"]

    def per_device(grad_terms, weights, basis, first_moment, second_moment):
        args = (grad_terms, weights, basis, first_moment, second_moment)
        if n_shard == 2 and n_tensor > 1:
            return fused_device(n_tensor, *args)
        return plain_device(*args)

    return jax.shard_map(
        per_device,
        mesh=mesh,
        in_specs=(
            P("section", "shard", "tensor", None),
            P("section", "tensor", "shard", None),
            P("section", None, None),
            P("section", "tensor", "shard", None),
            P("section", "tensor", "shard", None),
        ),
        out_specs=(
            P("section", "tensor", "shard", None),
            P("section", "tensor", "shard", None),
            P("section", "tensor", "shard", None),
            P("section", None, None),
        ),
        check_vma=False,
    )
```

```python
import functools
import math

import jax
import jax.numpy as jnp
from jax import lax
from jax.experimental import pallas as pl
from jax.experimental.pallas import tpu as pltpu
from jax.sharding import PartitionSpec as P

NS_STEPS = 5
MESH = pl.DeviceIdType.MESH
F32 = jnp.float32
BF16 = jnp.bfloat16
NN = ((1,), (0,))
NT = ((1,), (1,))
TILE = 256
SUBS = 2
SKEW = 3
VMEM_LIMIT = 56 * 1024 * 1024


def split(value):
    high = value.astype(BF16)
    return high, (value - high.astype(F32)).astype(BF16)


def dot3(left, right, dims):
    def one(a, b):
        return lax.dot_general(a, b, (dims, ((), ())), preferred_element_type=F32)

    return one(left[0], right[0]) + (one(left[0], right[1]) + one(left[1], right[0]))


def reduce_kernel(
    n_tensor,
    grad_hbm,
    basis_hbm,
    weight_hbm,
    first_hbm,
    second_hbm,
    weight_out,
    first_out,
    second_out,
    power_out,
    gram_out,
    grad,
    grad_high,
    grad_low,
    basis,
    basis_high,
    basis_low,
    low_mine,
    low_other,
    low_full,
    turned_high,
    turned_low,
    weight,
    first,
    second,
    part,
    part_other,
    own,
    pre_in,
    suf_in,
    pre_out,
    suf_out,
    total,
    in_sem,
    grad_sem,
    low_send,
    low_recv,
    part_send,
    part_recv,
    pre_send,
    pre_recv,
    suf_send,
    suf_recv,
    tot_send,
    tot_recv,
    out_sem,
):
    rows, width = grad.shape
    rank = basis.shape[1]
    half_rows = weight.shape[0]
    half_rank = rank // 2
    sub_rank = half_rank // SUBS
    row_tiles, col_tiles = rows // TILE, width // TILE
    pieces = col_tiles * SUBS
    root_width = math.sqrt(width)
    core = lax.axis_index("shard")
    other = 1 - core
    here = lax.axis_index("tensor")
    has_left, has_right = here > 0, here < n_tensor - 1

    def grad_copy(i):
        at = pl.ds(pl.multiple_of(i * TILE, TILE), TILE)
        return pltpu.make_async_copy(grad_hbm.at[at], grad.at[at], grad_sem.at[i])

    basis_copy = pltpu.make_async_copy(basis_hbm, basis, in_sem.at[0])
    basis_copy.start()
    for i in range(row_tiles):
        grad_copy(i).start()
    state_copies = [
        pltpu.make_async_copy(first_hbm, first, in_sem.at[1]),
        pltpu.make_async_copy(second_hbm, second, in_sem.at[2]),
        pltpu.make_async_copy(weight_hbm, weight, in_sem.at[3]),
    ]
    for copy in state_copies:
        copy.start()

    barrier = pltpu.get_barrier_semaphore()
    pl.semaphore_signal(barrier, inc=1, device_id={"shard": other}, device_id_type=MESH)

    @pl.when(has_left)
    def _():
        pl.semaphore_signal(barrier, inc=1, device_id={"tensor": here - 1}, device_id_type=MESH)

    @pl.when(has_right)
    def _():
        pl.semaphore_signal(barrier, inc=1, device_id={"tensor": here + 1}, device_id_type=MESH)

    basis_copy.wait()
    high, low = split(basis[...])
    basis_high[...] = high
    basis_low[...] = low

    pl.semaphore_wait(barrier, 1 + has_left.astype(jnp.int32) + has_right.astype(jnp.int32))

    def low_copy(i):
        at = pl.ds(pl.multiple_of(i * TILE, TILE), TILE)
        return pltpu.make_async_remote_copy(
            src_ref=low_mine.at[at],
            dst_ref=low_other.at[at],
            send_sem=low_send.at[i],
            recv_sem=low_recv.at[i],
            device_id={"shard": other},
            device_id_type=MESH,
        )

    def project(i, _):
        at = pl.ds(pl.multiple_of(i * TILE, TILE), TILE)
        grad_copy(i).wait()
        pair = split(grad[at, :])
        grad_high[at, :] = pair[0]
        grad_low[at, :] = pair[1]
        low_mine[at, :] = dot3(pair, (basis_high[...], basis_low[...]), NN)
        low_copy(i).start()
        return 0

    lax.fori_loop(0, row_tiles, project, 0)

    def join(i, _):
        at = pl.ds(pl.multiple_of(i * TILE, TILE), TILE)
        low_copy(i).wait_recv()
        block = (low_mine[at, :] + low_other[at, :]) * (1.0 / root_width)
        low_full[at, :] = block
        pair = split(block.T)
        turned_high[:, at] = pair[0]
        turned_low[:, at] = pair[1]
        return 0

    lax.fori_loop(0, row_tiles, join, 0)

    def part_copy(d):
        return pltpu.make_async_remote_copy(
            src_ref=part.at[d, pl.ds(pl.multiple_of(other * half_rank, half_rank), half_rank)],
            dst_ref=part_other.at[d],
            send_sem=part_send.at[d],
            recv_sem=part_recv.at[d],
            device_id={"shard": other},
            device_id_type=MESH,
        )

    def line_copy(source, target, k, send, recv, device):
        return pltpu.make_async_remote_copy(
            src_ref=source.at[k],
            dst_ref=target.at[k],
            send_sem=send.at[k],
            recv_sem=recv.at[k],
            device_id={"tensor": device},
            device_id_type=MESH,
        )

    def pre_copy(source, k):
        return line_copy(source, pre_in, k, pre_send, pre_recv, here + 1)

    def suf_copy(source, k):
        return line_copy(source, suf_in, k, suf_send, suf_recv, here - 1)

    def settle(d):
        part_copy(d).wait_recv()
        for s in range(SUBS):
            k = d * SUBS + s
            mine = pl.ds(pl.multiple_of(core * half_rank + s * sub_rank, sub_rank), sub_rank)
            own[k] = part[d, mine, :] + part_other[d, s * sub_rank : (s + 1) * sub_rank, :]

            @pl.when(jnp.logical_not(has_left))
            def _():
                pre_copy(own, k).start()

            @pl.when(jnp.logical_not(has_right))
            def _():
                suf_copy(own, k).start()

    def power_tile(d, _):
        at = pl.ds(pl.multiple_of(d * TILE, TILE), TILE)
        part[d] = dot3(
            (turned_high[...], turned_low[...]), (grad_high[:, at], grad_low[:, at]), NN
        )
        part_copy(d).start()

        @pl.when(d >= 1)
        def _():
            settle(d - 1)

        return 0

    lax.fori_loop(0, col_tiles, power_tile, 0)
    settle(col_tiles - 1)
    for copy in state_copies:
        copy.wait()

    def forward_pre(k):
        @pl.when(has_left)
        def _():
            pre_copy(pre_out, k).wait_recv()

            @pl.when(has_right)
            def _():
                pre_out[k] = pre_in[k] + own[k]
                pre_copy(pre_out, k).start()

    def forward_suf(k):
        @pl.when(has_right)
        def _():
            suf_copy(suf_out, k).wait_recv()

            @pl.when(has_left)
            def _():
                suf_out[k] = suf_in[k] + own[k]
                suf_copy(suf_out, k).start()

    def total_copy(k):
        d, s = k // SUBS, k % SUBS
        at = pl.ds(pl.multiple_of(core * half_rank + s * sub_rank, sub_rank), sub_rank)
        return pltpu.make_async_remote_copy(
            src_ref=total.at[d, at],
            dst_ref=total.at[d, at],
            send_sem=tot_send.at[k],
            recv_sem=tot_recv.at[k],
            device_id={"shard": other},
            device_id_type=MESH,
        )

    def finish(k):
        d, s = k // SUBS, k % SUBS
        at = pl.ds(pl.multiple_of(core * half_rank + s * sub_rank, sub_rank), sub_rank)

        @pl.when(jnp.logical_not(has_left))
        def _():
            total[d, at, :] = own[k] + suf_in[k]

        @pl.when(jnp.logical_not(has_right))
        def _():
            total[d, at, :] = own[k] + pre_in[k]

        @pl.when(jnp.logical_and(has_left, has_right))
        def _():
            total[d, at, :] = own[k] + (pre_in[k] + suf_in[k])

        total_copy(k).start()

    step_rows = half_rows // col_tiles

    def state_copy_out(source, target, j, which):
        at = pl.ds(pl.multiple_of(j * step_rows, 16), step_rows)
        return pltpu.make_async_copy(source.at[at], target.at[at], out_sem.at[which, j])

    def out_copies(j):
        return [
            state_copy_out(weight, weight_out, j, 0),
            state_copy_out(first, first_out, j, 1),
            state_copy_out(second, second_out, j, 2),
        ]

    def update_rows(j):
        at = pl.ds(pl.multiple_of(j * step_rows, 16), step_rows)
        low_rank = low_full[pl.ds(pl.multiple_of(core * half_rows + j * step_rows, 16), step_rows), :]
        moment_one = 0.9 * first[at, :] + 0.1 * low_rank
        moment_two = 0.95 * second[at, :] + 0.05 * low_rank * low_rank
        first[at, :] = moment_one
        second[at, :] = moment_two
        direction = moment_one / (jnp.sqrt(moment_two) + 1e-08)
        update = dot3(split(direction), (basis_high[...], basis_low[...]), NT)
        stepped = weight[at, :].astype(F32) - (0.5 / root_width) * update
        mean = jnp.mean(stepped * stepped, axis=1, keepdims=True)
        weight[at, :] = (stepped * lax.rsqrt(mean + 1e-06)).astype(BF16)
        for copy in out_copies(j):
            copy.start()

    gram_out[...] = jnp.zeros_like(gram_out)

    def gram_tile(d):
        for s in range(SUBS):
            total_copy(d * SUBS + s).wait_recv()
        block = total[d]
        pair = split(block)
        gram_out[...] += dot3(pair, pair, NT)
        power_out[pl.ds(pl.multiple_of(d * TILE, TILE), TILE), :] = block.T

    left_side = 2 * here < n_tensor

    def line_step(step, _):
        @pl.when(step < pieces)
        def _():
            @pl.when(left_side)
            def _():
                forward_pre(step)

            @pl.when(jnp.logical_not(left_side))
            def _():
                forward_suf(step)

        @pl.when(step >= SKEW)
        def _():
            k = step - SKEW

            @pl.when(left_side)
            def _():
                forward_suf(k)

            @pl.when(jnp.logical_not(left_side))
            def _():
                forward_pre(k)

            finish(k)

            @pl.when(jnp.logical_and(k % SUBS == SUBS - 1, k >= 2 * SUBS - 1))
            def _():
                gram_tile(k // SUBS - 1)

        @pl.when(jnp.logical_and(step % SUBS == 0, step < pieces))
        def _():
            pass

        return 0

    ends = jnp.logical_not(jnp.logical_and(has_left, has_right))

    def updates(j, _):
        update_rows(j)
        return 0

    @pl.when(ends)
    def _():
        lax.fori_loop(0, col_tiles, updates, 0)

    lax.fori_loop(0, pieces + SKEW, line_step, 0)

    @pl.when(jnp.logical_not(ends))
    def _():
        lax.fori_loop(0, col_tiles, updates, 0)

    gram_tile(col_tiles - 1)

    def drain(d, _):
        low_copy(d).wait_send()
        part_copy(d).wait_send()
        for copy in out_copies(d):
            copy.wait()
        for s in range(SUBS):
            k = d * SUBS + s
            total_copy(k).wait_send()

            @pl.when(has_right)
            def _():
                pre_copy(pre_out, k).wait_send()

            @pl.when(has_left)
            def _():
                suf_copy(suf_out, k).wait_send()

        return 0

    lax.fori_loop(0, col_tiles, drain, 0)


def newton_scale(gram, dot, between=None):
    size = gram.shape[0]
    rows = lax.broadcasted_iota(jnp.int32, (size, size), 0)
    columns = lax.broadcasted_iota(jnp.int32, (size, size), 1)
    eye = jnp.where(rows == columns, 1.0, 0.0).astype(F32)
    scaling = lax.rsqrt(jnp.sum(gram * eye) + 1e-06)
    now = gram * (scaling * scaling)
    product = None
    for sweep in range(NS_STEPS):
        factor = 1.5 * eye - 0.5 * now
        if sweep == 2 and between is not None:
            between()
        if sweep + 1 < NS_STEPS:
            now = dot(dot(now, factor), factor)
        product = factor if product is None else dot(product, factor)
    return product, scaling


def finish_kernel(
    power_ref, gram_ref, weight_in, first_in, second_in,
    weight_out, first_out, second_out, basis_out, weight, first, second, in_sem, out_sem,
):
    held = ((weight_in, weight, weight_out), (first_in, first, first_out), (second_in, second, second_out))
    loads = [pltpu.make_async_copy(a, b, in_sem.at[i]) for i, (a, b, _) in enumerate(held)]
    stores = [pltpu.make_async_copy(b, c, out_sem.at[i]) for i, (_, b, c) in enumerate(held)]
    for copy in loads:
        copy.start()

    def pass_on():
        for load, store in zip(loads, stores):
            load.wait()
            store.start()

    product, scaling = newton_scale(
        gram_ref[...], lambda a, b: dot3(split(a), split(b), NN), pass_on
    )
    product = split(product * (scaling * math.sqrt(power_ref.shape[0])))
    for d in range(power_ref.shape[0] // TILE):
        at = pl.ds(d * TILE, TILE)
        basis_out[at, :] = dot3(split(power_ref[at, :]), product, NN)
    for copy in stores:
        copy.wait()


def fused_device(n_tensor, grad_terms, weights, basis, first_moment, second_moment):
    rows, width = grad_terms.shape[2:]
    rank = basis.shape[2]
    half_rows = rows // 2
    tiles = width // TILE
    row_tiles = rows // TILE
    pieces = tiles * SUBS
    piece = (pieces, rank // 2 // SUBS, TILE)
    hbm = pl.BlockSpec(memory_space=pl.ANY)
    vmem = pl.BlockSpec(memory_space=pltpu.VMEM)
    dma = pltpu.SemaphoreType.DMA
    state = [
        jax.ShapeDtypeStruct((half_rows, width), BF16),
        jax.ShapeDtypeStruct((half_rows, rank), F32),
        jax.ShapeDtypeStruct((half_rows, rank), F32),
    ]
    new_weights, new_first, new_second, power, gram = pl.pallas_call(
        functools.partial(reduce_kernel, n_tensor),
        out_shape=state
        + [
            jax.ShapeDtypeStruct((width, rank), F32),
            jax.ShapeDtypeStruct((rank, rank), F32),
        ],
        in_specs=[hbm] * 5,
        out_specs=[hbm, hbm, hbm, vmem, vmem],
        scratch_shapes=[
            pltpu.VMEM((rows, width), F32),
            pltpu.VMEM((rows, width), BF16),
            pltpu.VMEM((rows, width), BF16),
            pltpu.VMEM((width, rank), F32),
            pltpu.VMEM((width, rank), BF16),
            pltpu.VMEM((width, rank), BF16),
            pltpu.VMEM((rows, rank), F32),
            pltpu.VMEM((rows, rank), F32),
            pltpu.VMEM((rows, rank), F32),
            pltpu.VMEM((rank, rows), BF16),
            pltpu.VMEM((rank, rows), BF16),
            pltpu.VMEM((half_rows, width), BF16),
            pltpu.VMEM((half_rows, rank), F32),
            pltpu.VMEM((half_rows, rank), F32),
            pltpu.VMEM((tiles, rank, TILE), F32),
            pltpu.VMEM((tiles, rank // 2, TILE), F32),
            pltpu.VMEM(piece, F32),
            pltpu.VMEM(piece, F32),
            pltpu.VMEM(piece, F32),
            pltpu.VMEM(piece, F32),
            pltpu.VMEM(piece, F32),
            pltpu.VMEM((tiles, rank, TILE), F32),
            dma((4,)),
            dma((row_tiles,)),
            dma((row_tiles,)),
            dma((row_tiles,)),
            dma((tiles,)),
            dma((tiles,)),
            dma((pieces,)),
            dma((pieces,)),
            dma((pieces,)),
            dma((pieces,)),
            dma((pieces,)),
            dma((pieces,)),
            dma((3, tiles)),
        ],
        compiler_params=pltpu.CompilerParams(
            collective_id=0, has_side_effects=True, vmem_limit_bytes=VMEM_LIMIT
        ),
        name="reduce",
    )(grad_terms[0, 0], basis[0], weights[0, 0], first_moment[0, 0], second_moment[0, 0])
    new_weights, new_first, new_second, new_basis = pl.pallas_call(
        finish_kernel,
        out_shape=state + [jax.ShapeDtypeStruct((width, rank), F32)],
        in_specs=[vmem, vmem, hbm, hbm, hbm],
        out_specs=[hbm, hbm, hbm, vmem],
        scratch_shapes=[
            pltpu.VMEM((half_rows, width), BF16),
            pltpu.VMEM((half_rows, rank), F32),
            pltpu.VMEM((half_rows, rank), F32),
            dma((3,)),
            dma((3,)),
        ],
        compiler_params=pltpu.CompilerParams(vmem_limit_bytes=VMEM_LIMIT),
        name="finish",
    )(power, gram, new_weights, new_first, new_second)
    return (
        new_weights[None, None],
        new_first[None, None],
        new_second[None, None],
        new_basis[None],
    )


def dot_high(left, right, dims=NN):
    return lax.dot_general(
        left, right, (dims, ((), ())), precision=lax.Precision.HIGH, preferred_element_type=F32
    )


def plain_device(grad_terms, weights, basis, first_moment, second_moment):
    basis_now = basis[0]
    root_width = math.sqrt(basis_now.shape[0])
    grad_rows = lax.psum_scatter(grad_terms[0, 0], "shard", scatter_dimension=0, tiled=True)
    low_rank = dot_high(grad_rows, basis_now) / root_width
    power_part = dot_high(grad_rows, low_rank, ((0,), (0,)))
    power = lax.psum(power_part, ("shard", "tensor"))
    moment_one = 0.9 * first_moment[0, 0] + 0.1 * low_rank
    moment_two = 0.95 * second_moment[0, 0] + 0.05 * low_rank * low_rank
    direction = moment_one / (jnp.sqrt(moment_two) + 1e-08)
    update = dot_high(direction, basis_now, NT)
    stepped = weights[0, 0].astype(F32) - 0.5 * update / root_width
    normed = stepped * lax.rsqrt(jnp.mean(stepped * stepped, axis=1, keepdims=True) + 1e-06)
    product, scaling = newton_scale(dot_high(power, power, ((0,), (0,))), dot_high)
    new_basis = dot_high(power, product) * (scaling * root_width)
    return (
        normed.astype(BF16)[None, None],
        moment_one[None, None],
        moment_two[None, None],
        new_basis[None],
    )


def solution(mesh):
    n_shard, n_tensor = mesh.shape["shard"], mesh.shape["tensor"]

    def per_device(grad_terms, weights, basis, first_moment, second_moment):
        args = (grad_terms, weights, basis, first_moment, second_moment)
        if n_shard == 2 and n_tensor > 1:
            return fused_device(n_tensor, *args)
        return plain_device(*args)

    return jax.shard_map(
        per_device,
        mesh=mesh,
        in_specs=(
            P("section", "shard", "tensor", None),
            P("section", "tensor", "shard", None),
            P("section", None, None),
            P("section", "tensor", "shard", None),
            P("section", "tensor", "shard", None),
        ),
        out_specs=(
            P("section", "tensor", "shard", None),
            P("section", "tensor", "shard", None),
            P("section", "tensor", "shard", None),
            P("section", None, None),
        ),
        check_vma=False,
    )
```
